32 devices in a mesh: row: 8 (over z, core), col: 2 (over y), lrn: 2 (over x).
Axes of the slice: x: 2, y: 2, z: 4, core: 2. Of those that a mesh axis runs over, the one named last changes fastest.
Arguments:
- responses: int32 [4096, 16384], P('lrn', ('row', 'col')), may hold values 0 or 1
- observed: int32 [4096, 16384], P('lrn', ('row', 'col')), may hold values from 0 to 1, as said below
- qmatrix: int32 [16384, 8], P(('row', 'col')), may hold values from 0 to 1
- guess: float32 [16384], P(('row', 'col')), may hold values from 0.05 to 0.35
- slip: float32 [16384], P(('row', 'col')), may hold values from 0.05 to 0.35
Outputs:
- q3_scaled: float32 [16384, 16384], P('row', ('col', 'lrn'))
The draws below stay inside these ranges and needn't reach their ends.
Inputs may be any that keep to these rules, and one draw needn't show every extreme that they name: Some items have no observed response from any learner.
All inputs are finite; a program needn't handle non-finite values. No bound on the sum of `responses` on one device may be relied on, other than what follows from the above.
Results may differ from the reference program's by a relative error of at most 0.008.
Values may be sent and summed in bfloat16 or wider, within the bound.
A program may use at most 192 MiB of HBM per device.

```python
import math
import jax
import jax.numpy as jnp
from jax import lax

J = 16384
ATTRS = 8
PROFILES = 256
LEARNERS = 4096


def draw_observed(key, part):
    learner = jnp.arange(LEARNERS, dtype=jnp.int32)
    threshold = 100 + 800 * learner // max(LEARNERS - 1, 1)
    rolls = jax.random.randint(jax.random.fold_in(key, 11), (LEARNERS, J), 0, 1000)
    base = rolls < threshold[:, None]
    silent = jax.random.randint(jax.random.fold_in(key, 12), (J,), 0, 64) == 0
    forced = jax.random.randint(jax.random.fold_in(key, 13), (), 0, J)
    silent = silent | (jnp.arange(J, dtype=jnp.int32) == forced)
    return jnp.where(silent[None, :], 0, base.astype(jnp.int32)).astype(jnp.int32)


def place_ends(result, stream_key, smallest, top_value):
    extent = result.shape
    place = [jax.random.randint(jax.random.fold_in(stream_key, axis), (), 0, extent[axis]) for axis in range(len(extent))]
    result = result.at[tuple(place)].set(smallest)
    longest = extent.index(max(extent))
    place[longest] = (place[longest] + 1) % extent[longest]
    return result.at[tuple(place)].set(top_value)


def steps_of(stream_key, extent, split, smallest, high):
    level, own = 1.0, jax.random.fold_in(stream_key, 6)
    for position, blocks in split:
        heights = jnp.exp(jax.random.uniform(jax.random.fold_in(own, position), (blocks,), jnp.float32, smallest / len(split), high / len(split)))
        level = level * jnp.repeat(heights, extent[position] // blocks).reshape([-1 if axis == position else 1 for axis in range(len(extent))])
    return level


def setup_inputs(seed: int = 0) -> dict:
    keys = jax.random.split(jax.random.key(seed), 6)
    responses = place_ends((jax.random.randint(keys[0], (LEARNERS, J), 0, 2) < 1).astype(jnp.int32), jax.random.fold_in(keys[0], 1), 0, 1)
    observed = draw_observed(jax.random.fold_in(keys[5], 71), 0)
    qmatrix = place_ends(jax.random.randint(keys[2], (J, ATTRS), 0, 2), jax.random.fold_in(keys[2], 1), 0, 1).astype(jnp.int32)
    guess = jnp.clip(jnp.exp(math.log(0.35) - 1.9459101 * jax.random.uniform(keys[3], (J,), jnp.float32) ** steps_of(keys[3], (J,), ((0, 16),), -0.2, 0.2)), 0.05, 0.35)
    slip = jnp.clip(jnp.exp(math.log(0.35) - 1.9459101 * jax.random.uniform(keys[4], (J,), jnp.float32) ** steps_of(keys[4], (J,), ((0, 16),), -0.2, 0.2)), 0.05, 0.35)
    return {"responses": responses, "observed": observed, "qmatrix": qmatrix, "guess": guess, "slip": slip}


def success(qmatrix, guess, slip):
    codes = jnp.arange(PROFILES, dtype=jnp.int32)
    powers = jnp.arange(ATTRS, dtype=jnp.int32)
    bits = (codes[None, :] >> powers[:, None] & 1).astype(jnp.float32)
    lacking = jnp.dot(qmatrix.astype(jnp.float32), 1.0 - bits, precision=lax.Precision.HIGHEST)
    return jnp.where(lacking == 0.0, 1.0 - slip[:, None], guess[:, None])

def reference(responses, observed, qmatrix, guess, slip):
    prob = success(qmatrix, guess, slip)
    answered = responses.astype(jnp.float32)
    seen = observed.astype(jnp.float32)
    loglik = jnp.dot(seen * answered, jnp.log(prob), precision=lax.Precision.HIGHEST)
    loglik = loglik + jnp.dot(seen * (1.0 - answered), jnp.log(1.0 - prob), precision=lax.Precision.HIGHEST)
    posterior = jax.nn.softmax(loglik, axis=1).astype(jnp.bfloat16)
    expected = jnp.dot(posterior, prob.astype(jnp.bfloat16).T, preferred_element_type=jnp.float32)
    resid = seen * (answered - expected)
    count = jnp.maximum(lax.optimization_barrier(jnp.sum(seen, axis=0)), 1.0)
    mean = lax.optimization_barrier(jnp.sum(resid, axis=0)) / count
    var = lax.optimization_barrier(jnp.sum(resid * resid, axis=0)) / count - mean * mean
    zres = (seen * (resid - mean) * lax.rsqrt(var + 1e-06) * lax.rsqrt(count)).astype(jnp.bfloat16)
    wide = zres.astype(jnp.float32)
    gram = jnp.dot(wide.T, wide, precision=lax.Precision.HIGHEST)
    return gram * jnp.sqrt(jnp.float32(LEARNERS))
```

```python
import functools

import jax
import jax.numpy as jnp
from jax import lax
from jax.experimental import pallas as pl
from jax.experimental.pallas import tpu as pltpu
from jax.sharding import PartitionSpec as P

ATTRS = 8
PROFILES = 256
CHUNK = 128
GROUP = 2 * CHUNK
TILE = 512
AHEAD = 3
MESH = pl.DeviceIdType.MESH


def spread(x, axis, root):
    mine = lax.axis_index(axis) == root
    return lax.psum(jnp.where(mine, x, jnp.zeros_like(x)), axis)


def mastered(qmatrix):
    codes = jnp.arange(PROFILES, dtype=jnp.int32)
    powers = jnp.arange(ATTRS, dtype=jnp.int32)
    bits = (codes[None, :] >> powers[:, None] & 1).astype(jnp.float32)
    lacking = jnp.dot(qmatrix.astype(jnp.float32), 1.0 - bits, precision=lax.Precision.HIGHEST)
    return lacking == 0.0


def learner_product(left, right):
    return lax.dot_general(
        left, right, (((0,), (0,)), ((), ())), preferred_element_type=jnp.float32
    )


def head(x):
    return lax.reduce_precision(x, 8, 7)


def residuals(responses, observed, qmatrix, guess, slip):
    full = mastered(qmatrix)
    prob = jnp.where(full, 1.0 - slip[:, None], guess[:, None])
    answered = responses.astype(jnp.float32)
    seen = observed.astype(jnp.float32)
    high = 1.0 - slip
    right = jnp.log(high) - jnp.log(guess)
    wrong = jnp.log(1.0 - high) - jnp.log(1.0 - guess)
    gain = seen * (answered * right + (1.0 - answered) * wrong)
    first = head(gain)
    second = head(gain - first)
    third = head(gain - first - second)
    select = full.astype(jnp.bfloat16)
    partial_value = sum(
        jnp.dot(part.astype(jnp.bfloat16), select, preferred_element_type=jnp.float32)
        for part in (third, second, first)
    )
    loglik = lax.psum_scatter(partial_value, ("row", "col"), scatter_dimension=0, tiled=True)
    posterior = jax.nn.softmax(loglik, axis=1).astype(jnp.bfloat16)
    posterior = lax.all_gather(posterior, ("row", "col"), axis=0, tiled=True)
    expected = jnp.dot(posterior, prob.astype(jnp.bfloat16).T, preferred_element_type=jnp.float32)
    resid = seen * (answered - expected)
    count, total, square = lax.psum(
        (jnp.sum(seen, axis=0), jnp.sum(resid, axis=0), jnp.sum(resid * resid, axis=0)), "lrn"
    )
    count = jnp.maximum(count, 1.0)
    mean = total / count
    var = square / count - mean * mean
    return (seen * (resid - mean) * lax.rsqrt(var + 1e-06) * lax.rsqrt(count)).astype(jnp.bfloat16)


def gram_kernel(planes, scale, z_ref, out_ref, panel, cols, stage, own_sem, out_sem,
                xs, xr, ys, yr, us, ds, zr, ss, sr):
    items = z_ref.shape[0]
    n = items // CHUNK
    r, c, l = lax.axis_index("row"), lax.axis_index("col"), lax.axis_index("lrn")
    plane, core = r // 2, r % 2
    line = c * 2 + l
    source = plane == line
    goes_up = (plane >= line) & (plane < planes - 1)
    goes_down = (plane <= line) & (plane > 0)
    x_to, y_to = (r, c, 1 - l), (r, 1 - c, l)
    up_to, down_to, twin = (r + 2, c, l), (r - 2, c, l), (r + 1 - 2 * core, c, l)

    barrier = pltpu.get_barrier_semaphore()
    for other in (x_to, y_to, twin):
        pl.semaphore_signal(barrier, inc=1, device_id=other, device_id_type=MESH)

    @pl.when(plane < planes - 1)
    def _():
        pl.semaphore_signal(barrier, inc=1, device_id=up_to, device_id_type=MESH)

    @pl.when(plane > 0)
    def _():
        pl.semaphore_signal(barrier, inc=1, device_id=down_to, device_id_type=MESH)

    ends = jnp.where(plane == 0, 1, 0) + jnp.where(plane == planes - 1, 1, 0)
    pl.semaphore_wait(barrier, 5 - ends)

    own = pltpu.make_async_copy(z_ref, panel.at[l, c], own_sem)
    own.start()
    own.wait()

    def rows(i):
        return pl.ds(pl.multiple_of(i * CHUNK, CHUNK), CHUNK)

    def remote(src, dst, send, recv, to):
        return pltpu.make_async_remote_copy(
            src_ref=src, dst_ref=dst, send_sem=send, recv_sem=recv,
            device_id=to, device_id_type=MESH,
        )

    def x_copy(far, i):
        ref = panel.at[l, (1 - c) if far else c, rows(i)]
        at = i + n * far
        return remote(ref, ref, xs.at[at], xr.at[at], x_to)

    def x_wait(far, i):
        ref = panel.at[1 - l, (1 - c) if far else c, rows(i)]
        at = i + n * far
        remote(ref, ref, xs.at[at], xr.at[at], x_to).wait_recv()

    def y_copy(i):
        ref = panel.at[l, c, rows(i)]
        return remote(ref, ref, ys.at[i], yr.at[i], y_to)

    def y_wait(i):
        ref = panel.at[l, 1 - c, rows(i)]
        remote(ref, ref, ys.at[i], yr.at[i], y_to).wait_recv()

    def place(q):
        far, i, cross = q // (2 * n), (q % (2 * n)) // 2, q % 2
        return l + cross - 2 * l * cross, c + far - 2 * c * far, i

    def chunk(which, q):
        px, py, i = place(q)
        return cols.at[which, px, py, rows(i)]

    def up_copy(q):
        return remote(chunk(core, q), chunk(core, q), us.at[q], zr.at[q], up_to)

    def down_copy(q):
        return remote(chunk(core, q), chunk(core, q), ds.at[q], zr.at[q], down_to)

    def twin_copy(q):
        return remote(chunk(core, q), chunk(core, q), ss.at[q], sr.at[q], twin)

    def sent(q):
        @pl.when(goes_up)
        def _():
            up_copy(q).wait_send()

        @pl.when(goes_down)
        def _():
            down_copy(q).wait_send()

        twin_copy(q).wait_send()

    def relay(q):
        @pl.when(source)
        def _():
            px, py, i = place(q)
            move = pltpu.make_async_copy(panel.at[px, py, rows(i)], chunk(core, q), own_sem)
            move.start()
            move.wait()

        @pl.when(jnp.logical_not(source))
        def _():
            up_copy(q).wait_recv()

        @pl.when(q >= AHEAD)
        def _():
            sent(q - AHEAD)

        @pl.when(goes_up)
        def _():
            up_copy(q).start()

        @pl.when(goes_down)
        def _():
            down_copy(q).start()

        twin_copy(q).start()

    def out_copy(slot, start):
        return pltpu.make_async_copy(
            stage.at[slot], out_ref.at[:, pl.ds(pl.multiple_of(start, GROUP), GROUP)],
            out_sem.at[slot],
        )

    def job(j):
        g, swap, slot = j // 2, j % 2, j % 2
        which = core + swap - 2 * core * swap

        @pl.when(swap == 1)
        def _():
            for s in range(4):
                q = 4 * g + s
                remote(chunk(which, q), chunk(which, q), ss.at[q], sr.at[q], twin).wait_recv()

        far = g // (n // 2)
        py = c + far - 2 * c * far
        base = pl.multiple_of((g % (n // 2)) * GROUP, GROUP)

        @pl.when(j >= 2)
        def _():
            out_copy(slot, 0).wait()

        per = items // TILE

        @pl.loop(0, 2 * per)
        def _(m):
            y2, off = m // per, pl.multiple_of((m % per) * TILE, TILE)
            acc = None
            for px in range(2):
                term = lax.dot_general(
                    panel[px, y2, pl.ds(off, TILE), :],
                    cols[which, px, py, pl.ds(base, GROUP), :],
                    (((1,), (1,)), ((), ())), preferred_element_type=jnp.float32,
                )
                acc = term if acc is None else acc + term
            stage[slot, pl.ds(pl.multiple_of(m * TILE, TILE), TILE), :] = acc * scale

        out_copy(slot, which * 2 * items + py * items + base).start()

    @pl.loop(0, 2 * n)
    def _(q):
        @pl.when(q < n)
        def _():
            x_copy(0, q).start()
            y_copy(q).start()

        @pl.when(q >= n)
        def _():
            y_wait(q - n)
            x_copy(1, q - n).start()

        @pl.when(q % 2 == 1)
        def _():
            x_wait(0, q // 2)

        relay(q)

    @pl.loop(0, n)
    def _(i):
        x_wait(1, i)

    @pl.loop(2 * n, 4 * n)
    def _(q):
        relay(q)

        @pl.when(q > 2 * n)
        def _():
            job(q - 2 * n - 1)

    job(2 * n - 1)

    @pl.loop(4 * n - AHEAD, 4 * n)
    def _(q):
        sent(q)

    @pl.loop(0, n)
    def _(i):
        x_copy(0, i).wait_send()
        x_copy(1, i).wait_send()
        y_copy(i).wait_send()

    out_copy(0, 0).wait()
    out_copy(1, 0).wait()


def line_gram(planes, scale, z):
    items, half = z.shape
    n = items // CHUNK
    dma = pltpu.SemaphoreType.DMA
    return pl.pallas_call(
        functools.partial(gram_kernel, planes, scale),
        out_shape=jax.ShapeDtypeStruct((2 * items, 4 * items), jnp.float32),
        in_specs=[pl.BlockSpec(memory_space=pl.ANY)],
        out_specs=pl.BlockSpec(memory_space=pl.ANY),
        scratch_shapes=[
            pltpu.VMEM((2, 2, items, half), jnp.bfloat16),
            pltpu.VMEM((2, 2, 2, items, half), jnp.bfloat16),
            pltpu.VMEM((2, 2 * items, GROUP), jnp.float32),
            dma, dma((2,)),
            dma((2 * n,)), dma((2 * n,)), dma((n,)), dma((n,)),
            dma((4 * n,)), dma((4 * n,)), dma((4 * n,)), dma((4 * n,)), dma((4 * n,)),
        ],
        compiler_params=pltpu.CompilerParams(
            collective_id=0, has_side_effects=True, vmem_limit_bytes=60 * 2**20
        ),
        cost_estimate=pl.CostEstimate(
            flops=2 * 2 * items * 4 * items * 2 * half,
            bytes_accessed=4 * 8 * items * items, transcendentals=0,
        ),
    )(z)


def shards(responses, observed, qmatrix, guess, slip):
    zres = residuals(responses, observed, qmatrix, guess, slip)
    learner_total = zres.shape[0] * lax.axis_size("lrn")
    tiles = lax.axis_size("col") * lax.axis_size("lrn")
    repeats = lax.axis_size("row") // tiles
    if lax.axis_size("col") == 2 and lax.axis_size("lrn") == 2 and repeats == 2:
        return line_gram(tiles, float(learner_total) ** 0.5, zres.T)
    panel = lax.all_gather(zres, "col", axis=1, tiled=True)
    whole_panel = lax.all_gather(panel, "lrn", axis=0, tiled=True)
    tile_index = lax.axis_index("col") * lax.axis_size("lrn") + lax.axis_index("lrn")
    pieces = [
        spread(whole_panel, "row", tile_index * repeats + offset) for offset in range(repeats)
    ]
    columns = jnp.concatenate(pieces, axis=1)
    gram = learner_product(whole_panel, columns)
    return gram * jnp.sqrt(jnp.float32(learner_total))


def solution(mesh):
    placed = (
        P("lrn", ("row", "col")),
        P("lrn", ("row", "col")),
        P(("row", "col"), None),
        P(("row", "col")),
        P(("row", "col")),
    )
    return jax.shard_map(
        shards, mesh=mesh, in_specs=placed, out_specs=P("row", ("col", "lrn")), check_vma=False
    )
```

```python
import functools

import jax
import jax.numpy as jnp
from jax import lax
from jax.experimental import pallas as pl
from jax.experimental.layout import Layout, with_layout_constraint
from jax.experimental.pallas import tpu as pltpu
from jax.sharding import PartitionSpec as P

ATTRS = 8
PROFILES = 256
CHUNK = 128
GROUP = 2 * CHUNK
TILE = 512
AHEAD = 3
MESH = pl.DeviceIdType.MESH


def spread(x, axis, root):
    mine = lax.axis_index(axis) == root
    return lax.psum(jnp.where(mine, x, jnp.zeros_like(x)), axis)


def mastered(qmatrix):
    codes = jnp.arange(PROFILES, dtype=jnp.int32)
    powers = jnp.arange(ATTRS, dtype=jnp.int32)
    bits = (codes[None, :] >> powers[:, None] & 1).astype(jnp.float32)
    lacking = jnp.dot(qmatrix.astype(jnp.float32), 1.0 - bits, precision=lax.Precision.HIGHEST)
    return lacking == 0.0


def learner_product(left, right):
    return lax.dot_general(
        left, right, (((0,), (0,)), ((), ())), preferred_element_type=jnp.float32
    )


def head(x):
    return lax.reduce_precision(x, 8, 7)


def compact():
    sizes = [lax.axis_size(axis) for axis in ("row", "col", "lrn")]
    return sizes == [8, 2, 2]


def posterior_kernel(planes, p_ref, out_ref, from_twin, from_y, from_z, sums,
                     send, recv, z_send, z_recv, g_send, g_recv):
    learners = p_ref.shape[0]
    half, quarter = learners // 2, learners // 4
    piece = quarter // planes
    r, c, l = lax.axis_index("row"), lax.axis_index("col"), lax.axis_index("lrn")
    plane, core = r // 2, r % 2
    twin, y_to = (r + 1 - 2 * core, c, l), (r, 1 - c, l)

    def z_to(step):
        there = lax.rem(plane + step, planes)
        return there, (2 * there + core, c, l)

    barrier = pltpu.get_barrier_semaphore()
    pl.semaphore_signal(barrier, inc=1, device_id=twin, device_id_type=MESH)
    pl.semaphore_signal(barrier, inc=1, device_id=y_to, device_id_type=MESH)
    for step in range(1, planes):
        pl.semaphore_signal(barrier, inc=1, device_id=z_to(step)[1], device_id_type=MESH)
    pl.semaphore_wait(barrier, 1 + planes)

    def span(start, size):
        return pl.ds(pl.multiple_of(start, piece), size)

    def remote(src, dst, send_sem, recv_sem, to):
        return pltpu.make_async_remote_copy(
            src_ref=src, dst_ref=dst, send_sem=send_sem, recv_sem=recv_sem,
            device_id=to, device_id_type=MESH,
        )

    first = remote(p_ref.at[span((1 - core) * half, half)], from_twin, send.at[0], recv.at[0], twin)
    first.start()
    first.wait()
    sums[...] = p_ref[span(core * half, half), :] + from_twin[...]

    second = remote(sums.at[span((1 - c) * quarter, quarter)], from_y, send.at[1], recv.at[1], y_to)
    second.start()
    second.wait()
    mine = span(c * quarter, quarter)
    sums[mine, :] = sums[mine, :] + from_y[...]

    thirds = []
    for step in range(1, planes):
        there, to = z_to(step)
        copy = remote(
            sums.at[span(c * quarter + there * piece, piece)], from_z.at[step - 1],
            z_send.at[step - 1], z_recv.at[step - 1], to,
        )
        copy.start()
        thirds.append(copy)
    for copy in thirds:
        copy.wait()
    loglik = sums[span(c * quarter + plane * piece, piece), :]
    for step in range(1, planes):
        loglik = loglik + from_z[step - 1]
    weight = jnp.exp(loglik - jnp.max(loglik, axis=1, keepdims=True))
    weight = weight / jnp.sum(weight, axis=1, keepdims=True)
    base = core * half + c * quarter
    own = span(base + plane * piece, piece)
    out_ref[own, :] = weight.astype(out_ref.dtype)

    copies = []
    for step in range(1, planes):
        copy = remote(
            out_ref.at[own], out_ref.at[own], g_send.at[step - 1], g_recv.at[step - 1],
            z_to(step)[1],
        )
        copy.start()
        copies.append(copy)
    for step in range(1, planes):
        copies[step - 1].wait_send()
        came = lax.rem(plane + planes - step, planes)
        block = out_ref.at[span(base + came * piece, piece)]
        remote(
            block, block, g_send.at[step - 1], g_recv.at[step - 1], z_to(step)[1]
        ).wait_recv()

    block = out_ref.at[span(base, quarter)]
    along = remote(block, block, send.at[2], recv.at[2], y_to)
    along.start()
    along.wait_send()
    block = out_ref.at[span(core * half + (1 - c) * quarter, quarter)]
    remote(block, block, send.at[2], recv.at[2], y_to).wait_recv()

    block = out_ref.at[span(core * half, half)]
    across = remote(block, block, send.at[3], recv.at[3], twin)
    across.start()
    across.wait_send()
    block = out_ref.at[span((1 - core) * half, half)]
    remote(block, block, send.at[3], recv.at[3], twin).wait_recv()


def shared_posterior(planes, partial_value):
    learners, profiles = partial_value.shape
    dma = pltpu.SemaphoreType.DMA
    f32 = jnp.float32
    return pl.pallas_call(
        functools.partial(posterior_kernel, planes),
        out_shape=jax.ShapeDtypeStruct((learners, profiles), jnp.bfloat16),
        in_specs=[pl.BlockSpec(memory_space=pltpu.VMEM)],
        out_specs=pl.BlockSpec(memory_space=pltpu.VMEM),
        scratch_shapes=[
            pltpu.VMEM((learners // 2, profiles), f32),
            pltpu.VMEM((learners // 4, profiles), f32),
            pltpu.VMEM((planes - 1, learners // 4 // planes, profiles), f32),
            pltpu.VMEM((learners // 2, profiles), f32),
            dma((4,)), dma((4,)),
            dma((planes - 1,)), dma((planes - 1,)), dma((planes - 1,)), dma((planes - 1,)),
        ],
        compiler_params=pltpu.CompilerParams(
            collective_id=1, has_side_effects=True, vmem_limit_bytes=32 * 2**20
        ),
    )(partial_value)


def residuals(responses, observed, qmatrix, guess, slip):
    full = mastered(qmatrix)
    prob = jnp.where(full, 1.0 - slip[:, None], guess[:, None])
    answered = responses.astype(jnp.float32)
    seen = observed.astype(jnp.float32)
    high = 1.0 - slip
    right = jnp.log(high) - jnp.log(guess)
    wrong = jnp.log(1.0 - high) - jnp.log(1.0 - guess)
    gain = seen * (answered * right + (1.0 - answered) * wrong)
    first = head(gain)
    second = head(gain - first)
    third = head(gain - first - second)
    select = full.astype(jnp.bfloat16)
    partial_value = sum(
        jnp.dot(part.astype(jnp.bfloat16), select, preferred_element_type=jnp.float32)
        for part in (third, second, first)
    )
    if compact():
        posterior = shared_posterior(lax.axis_size("row") // 2, partial_value)
    else:
        loglik = lax.psum_scatter(partial_value, ("row", "col"), scatter_dimension=0, tiled=True)
        posterior = jax.nn.softmax(loglik, axis=1).astype(jnp.bfloat16)
        posterior = lax.all_gather(posterior, ("row", "col"), axis=0, tiled=True)
    expected = jnp.dot(posterior, prob.astype(jnp.bfloat16).T, preferred_element_type=jnp.float32)
    resid = seen * (answered - expected)
    count, total, square = lax.psum(
        (jnp.sum(seen, axis=0), jnp.sum(resid, axis=0), jnp.sum(resid * resid, axis=0)), "lrn"
    )
    count = jnp.maximum(count, 1.0)
    mean = total / count
    var = square / count - mean * mean
    return (seen * (resid - mean) * lax.rsqrt(var + 1e-06) * lax.rsqrt(count)).astype(jnp.bfloat16)


def gram_kernel(planes, scale, z_ref, out_ref, panel, cols, stage, own_sem, out_sem,
                xs, xr, ys, yr, us, ds, zr, ss, sr):
    items = z_ref.shape[0]
    n = items // CHUNK
    r, c, l = lax.axis_index("row"), lax.axis_index("col"), lax.axis_index("lrn")
    plane, core = r // 2, r % 2
    line = c * 2 + l
    source = plane == line
    goes_up = (plane >= line) & (plane < planes - 1)
    goes_down = (plane <= line) & (plane > 0)
    x_to, y_to = (r, c, 1 - l), (r, 1 - c, l)
    up_to, down_to, twin = (r + 2, c, l), (r - 2, c, l), (r + 1 - 2 * core, c, l)

    barrier = pltpu.get_barrier_semaphore()
    for other in (x_to, y_to, twin):
        pl.semaphore_signal(barrier, inc=1, device_id=other, device_id_type=MESH)

    @pl.when(plane < planes - 1)
    def _():
        pl.semaphore_signal(barrier, inc=1, device_id=up_to, device_id_type=MESH)

    @pl.when(plane > 0)
    def _():
        pl.semaphore_signal(barrier, inc=1, device_id=down_to, device_id_type=MESH)

    ends = jnp.where(plane == 0, 1, 0) + jnp.where(plane == planes - 1, 1, 0)
    pl.semaphore_wait(barrier, 5 - ends)

    own = pltpu.make_async_copy(z_ref, panel.at[l, c], own_sem)
    own.start()
    own.wait()

    def rows(i):
        return pl.ds(pl.multiple_of(i * CHUNK, CHUNK), CHUNK)

    def remote(src, dst, send, recv, to):
        return pltpu.make_async_remote_copy(
            src_ref=src, dst_ref=dst, send_sem=send, recv_sem=recv,
            device_id=to, device_id_type=MESH,
        )

    def x_copy(far, i):
        ref = panel.at[l, (1 - c) if far else c, rows(i)]
        at = i + n * far
        return remote(ref, ref, xs.at[at], xr.at[at], x_to)

    def x_wait(far, i):
        ref = panel.at[1 - l, (1 - c) if far else c, rows(i)]
        at = i + n * far
        remote(ref, ref, xs.at[at], xr.at[at], x_to).wait_recv()

    def y_copy(i):
        ref = panel.at[l, c, rows(i)]
        return remote(ref, ref, ys.at[i], yr.at[i], y_to)

    def y_wait(i):
        ref = panel.at[l, 1 - c, rows(i)]
        remote(ref, ref, ys.at[i], yr.at[i], y_to).wait_recv()

    def place(q):
        far, i, cross = q // (2 * n), (q % (2 * n)) // 2, q % 2
        return l + cross - 2 * l * cross, c + far - 2 * c * far, i

    def chunk(which, q):
        px, py, i = place(q)
        return cols.at[which, px, py, rows(i)]

    def up_copy(q):
        return remote(chunk(core, q), chunk(core, q), us.at[q], zr.at[q], up_to)

    def down_copy(q):
        return remote(chunk(core, q), chunk(core, q), ds.at[q], zr.at[q], down_to)

    def twin_copy(q):
        return remote(chunk(core, q), chunk(core, q), ss.at[q], sr.at[q], twin)

    def sent(q):
        @pl.when(goes_up)
        def _():
            up_copy(q).wait_send()

        @pl.when(goes_down)
        def _():
            down_copy(q).wait_send()

        twin_copy(q).wait_send()

    def relay(q):
        @pl.when(source)
        def _():
            px, py, i = place(q)
            move = pltpu.make_async_copy(panel.at[px, py, rows(i)], chunk(core, q), own_sem)
            move.start()
            move.wait()

        @pl.when(jnp.logical_not(source))
        def _():
            up_copy(q).wait_recv()

        @pl.when(q >= AHEAD)
        def _():
            sent(q - AHEAD)

        @pl.when(goes_up)
        def _():
            up_copy(q).start()

        @pl.when(goes_down)
        def _():
            down_copy(q).start()

        twin_copy(q).start()

    def out_copy(slot, start):
        return pltpu.make_async_copy(
            stage.at[slot], out_ref.at[:, pl.ds(pl.multiple_of(start, GROUP), GROUP)],
            out_sem.at[slot],
        )

    def job(j):
        g, swap, slot = j // 2, j % 2, j % 2
        which = core + swap - 2 * core * swap

        @pl.when(swap == 1)
        def _():
            for s in range(4):
                q = 4 * g + s
                remote(chunk(which, q), chunk(which, q), ss.at[q], sr.at[q], twin).wait_recv()

        far = g // (n // 2)
        py = c + far - 2 * c * far
        base = pl.multiple_of((g % (n // 2)) * GROUP, GROUP)

        @pl.when(j >= 2)
        def _():
            out_copy(slot, 0).wait()

        per = items // TILE

        @pl.loop(0, 2 * per)
        def _(m):
            y2, off = m // per, pl.multiple_of((m % per) * TILE, TILE)
            acc = None
            for px in range(2):
                term = lax.dot_general(
                    panel[px, y2, pl.ds(off, TILE), :],
                    cols[which, px, py, pl.ds(base, GROUP), :],
                    (((1,), (1,)), ((), ())), preferred_element_type=jnp.float32,
                )
                acc = term if acc is None else acc + term
            stage[slot, pl.ds(pl.multiple_of(m * TILE, TILE), TILE), :] = acc * scale

        out_copy(slot, which * 2 * items + py * items + base).start()

    @pl.loop(0, 2 * n)
    def _(q):
        @pl.when(q < n)
        def _():
            x_copy(0, q).start()
            y_copy(q).start()

        @pl.when(q >= n)
        def _():
            y_wait(q - n)
            x_copy(1, q - n).start()

        @pl.when(q % 2 == 1)
        def _():
            x_wait(0, q // 2)

        relay(q)

    @pl.loop(0, n)
    def _(i):
        x_wait(1, i)

    @pl.loop(2 * n, 4 * n)
    def _(q):
        relay(q)

        @pl.when(q > 2 * n)
        def _():
            job(q - 2 * n - 1)

    job(2 * n - 1)

    @pl.loop(4 * n - AHEAD, 4 * n)
    def _(q):
        sent(q)

    @pl.loop(0, n)
    def _(i):
        x_copy(0, i).wait_send()
        x_copy(1, i).wait_send()
        y_copy(i).wait_send()

    out_copy(0, 0).wait()
    out_copy(1, 0).wait()


def line_gram(planes, scale, z):
    items, half = z.shape
    n = items // CHUNK
    dma = pltpu.SemaphoreType.DMA
    return pl.pallas_call(
        functools.partial(gram_kernel, planes, scale),
        out_shape=jax.ShapeDtypeStruct((2 * items, 4 * items), jnp.float32),
        in_specs=[pl.BlockSpec(memory_space=pl.ANY)],
        out_specs=pl.BlockSpec(memory_space=pl.ANY),
        scratch_shapes=[
            pltpu.VMEM((2, 2, items, half), jnp.bfloat16),
            pltpu.VMEM((2, 2, 2, items, half), jnp.bfloat16),
            pltpu.VMEM((2, 2 * items, GROUP), jnp.float32),
            dma, dma((2,)),
            dma((2 * n,)), dma((2 * n,)), dma((n,)), dma((n,)),
            dma((4 * n,)), dma((4 * n,)), dma((4 * n,)), dma((4 * n,)), dma((4 * n,)),
        ],
        compiler_params=pltpu.CompilerParams(
            collective_id=0, has_side_effects=True, vmem_limit_bytes=60 * 2**20
        ),
        cost_estimate=pl.CostEstimate(
            flops=2 * 2 * items * 4 * items * 2 * half,
            bytes_accessed=4 * 8 * items * items, transcendentals=0,
        ),
    )(z)


def shards(responses, observed, qmatrix, guess, slip):
    zres = residuals(responses, observed, qmatrix, guess, slip)
    learner_total = zres.shape[0] * lax.axis_size("lrn")
    tiles = lax.axis_size("col") * lax.axis_size("lrn")
    repeats = lax.axis_size("row") // tiles
    if compact():
        zres = with_layout_constraint(zres, Layout(major_to_minor=(0, 1)))
        return line_gram(tiles, float(learner_total) ** 0.5, zres.T)
    panel = lax.all_gather(zres, "col", axis=1, tiled=True)
    whole_panel = lax.all_gather(panel, "lrn", axis=0, tiled=True)
    tile_index = lax.axis_index("col") * lax.axis_size("lrn") + lax.axis_index("lrn")
    pieces = [
        spread(whole_panel, "row", tile_index * repeats + offset) for offset in range(repeats)
    ]
    columns = jnp.concatenate(pieces, axis=1)
    gram = learner_product(whole_panel, columns)
    return gram * jnp.sqrt(jnp.float32(learner_total))


def solution(mesh):
    placed = (
        P("lrn", ("row", "col")),
        P("lrn", ("row", "col")),
        P(("row", "col"), None),
        P(("row", "col")),
        P(("row", "col")),
    )
    return jax.shard_map(
        shards, mesh=mesh, in_specs=placed, out_specs=P("row", ("col", "lrn")), check_vma=False
    )
```

```python
import functools

import jax
import jax.numpy as jnp
from jax import lax
from jax.experimental import pallas as pl
from jax.experimental.layout import Layout, with_layout_constraint
from jax.experimental.pallas import tpu as pltpu
from jax.sharding import PartitionSpec as P

ATTRS = 8
PROFILES = 256
CHUNK = 64
GROUP = 256
PARTS = 2
TILE = 512
AHEAD = 4
MESH = pl.DeviceIdType.MESH


def spread(x, axis, root):
    mine = lax.axis_index(axis) == root
    return lax.psum(jnp.where(mine, x, jnp.zeros_like(x)), axis)


def mastered(qmatrix):
    codes = jnp.arange(PROFILES, dtype=jnp.int32)
    powers = jnp.arange(ATTRS, dtype=jnp.int32)
    bits = (codes[None, :] >> powers[:, None] & 1).astype(jnp.float32)
    lacking = jnp.dot(qmatrix.astype(jnp.float32), 1.0 - bits, precision=lax.Precision.HIGHEST)
    return lacking == 0.0


def learner_product(left, right):
    return lax.dot_general(
        left, right, (((0,), (0,)), ((), ())), preferred_element_type=jnp.float32
    )


def head(x):
    return lax.reduce_precision(x, 8, 7)


def compact():
    sizes = [lax.axis_size(axis) for axis in ("row", "col", "lrn")]
    return sizes == [8, 2, 2]


def posterior_kernel(planes, p_ref, out_ref, from_twin, from_y, from_z, sums,
                     send, recv, z_send, z_recv, g_send, g_recv):
    learners = p_ref.shape[0]
    half, quarter = learners // 2, learners // 4
    piece = quarter // planes
    r, c, l = lax.axis_index("row"), lax.axis_index("col"), lax.axis_index("lrn")
    plane, core = r // 2, r % 2
    twin, y_to = (r + 1 - 2 * core, c, l), (r, 1 - c, l)

    def z_to(step):
        there = lax.rem(plane + step, planes)
        return there, (2 * there + core, c, l)

    barrier = pltpu.get_barrier_semaphore()
    pl.semaphore_signal(barrier, inc=1, device_id=twin, device_id_type=MESH)
    pl.semaphore_signal(barrier, inc=1, device_id=y_to, device_id_type=MESH)
    for step in range(1, planes):
        pl.semaphore_signal(barrier, inc=1, device_id=z_to(step)[1], device_id_type=MESH)
    pl.semaphore_wait(barrier, 1 + planes)

    def span(start, size):
        return pl.ds(pl.multiple_of(start, piece), size)

    def remote(src, dst, send_sem, recv_sem, to):
        return pltpu.make_async_remote_copy(
            src_ref=src, dst_ref=dst, send_sem=send_sem, recv_sem=recv_sem,
            device_id=to, device_id_type=MESH,
        )

    first = remote(p_ref.at[span((1 - core) * half, half)], from_twin, send.at[0], recv.at[0], twin)
    first.start()
    first.wait()
    sums[...] = p_ref[span(core * half, half), :] + from_twin[...]

    second = remote(sums.at[span((1 - c) * quarter, quarter)], from_y, send.at[1], recv.at[1], y_to)
    second.start()
    second.wait()
    mine = span(c * quarter, quarter)
    sums[mine, :] = sums[mine, :] + from_y[...]

    thirds = []
    for step in range(1, planes):
        there, to = z_to(step)
        copy = remote(
            sums.at[span(c * quarter + there * piece, piece)], from_z.at[step - 1],
            z_send.at[step - 1], z_recv.at[step - 1], to,
        )
        copy.start()
        thirds.append(copy)
    for copy in thirds:
        copy.wait()
    loglik = sums[span(c * quarter + plane * piece, piece), :]
    for step in range(1, planes):
        loglik = loglik + from_z[step - 1]
    weight = jnp.exp(loglik - jnp.max(loglik, axis=1, keepdims=True))
    weight = weight / jnp.sum(weight, axis=1, keepdims=True)
    base = core * half + c * quarter
    own = span(base + plane * piece, piece)
    out_ref[own, :] = weight.astype(out_ref.dtype)

    copies = []
    for step in range(1, planes):
        copy = remote(
            out_ref.at[own], out_ref.at[own], g_send.at[step - 1], g_recv.at[step - 1],
            z_to(step)[1],
        )
        copy.start()
        copies.append(copy)
    for step in range(1, planes):
        copies[step - 1].wait_send()
        came = lax.rem(plane + planes - step, planes)
        block = out_ref.at[span(base + came * piece, piece)]
        remote(
            block, block, g_send.at[step - 1], g_recv.at[step - 1], z_to(step)[1]
        ).wait_recv()

    block = out_ref.at[span(base, quarter)]
    along = remote(block, block, send.at[2], recv.at[2], y_to)
    along.start()
    along.wait_send()
    block = out_ref.at[span(core * half + (1 - c) * quarter, quarter)]
    remote(block, block, send.at[2], recv.at[2], y_to).wait_recv()

    block = out_ref.at[span(core * half, half)]
    across = remote(block, block, send.at[3], recv.at[3], twin)
    across.start()
    across.wait_send()
    block = out_ref.at[span((1 - core) * half, half)]
    remote(block, block, send.at[3], recv.at[3], twin).wait_recv()


def shared_posterior(planes, partial_value):
    learners, profiles = partial_value.shape
    dma = pltpu.SemaphoreType.DMA
    f32 = jnp.float32
    return pl.pallas_call(
        functools.partial(posterior_kernel, planes),
        out_shape=jax.ShapeDtypeStruct((learners, profiles), jnp.bfloat16),
        in_specs=[pl.BlockSpec(memory_space=pltpu.VMEM)],
        out_specs=pl.BlockSpec(memory_space=pltpu.VMEM),
        scratch_shapes=[
            pltpu.VMEM((learners // 2, profiles), f32),
            pltpu.VMEM((learners // 4, profiles), f32),
            pltpu.VMEM((planes - 1, learners // 4 // planes, profiles), f32),
            pltpu.VMEM((learners // 2, profiles), f32),
            dma((4,)), dma((4,)),
            dma((planes - 1,)), dma((planes - 1,)), dma((planes - 1,)), dma((planes - 1,)),
        ],
        compiler_params=pltpu.CompilerParams(
            collective_id=1, has_side_effects=True, vmem_limit_bytes=32 * 2**20
        ),
    )(partial_value)


def residuals(responses, observed, qmatrix, guess, slip):
    full = mastered(qmatrix)
    prob = jnp.where(full, 1.0 - slip[:, None], guess[:, None])
    answered = responses.astype(jnp.float32)
    seen = observed.astype(jnp.float32)
    high = 1.0 - slip
    right = jnp.log(high) - jnp.log(guess)
    wrong = jnp.log(1.0 - high) - jnp.log(1.0 - guess)
    gain = seen * (answered * right + (1.0 - answered) * wrong)
    first = head(gain)
    second = head(gain - first)
    third = head(gain - first - second)
    select = full.astype(jnp.bfloat16)
    partial_value = sum(
        jnp.dot(part.astype(jnp.bfloat16), select, preferred_element_type=jnp.float32)
        for part in (third, second, first)
    )
    if compact():
        posterior = shared_posterior(lax.axis_size("row") // 2, partial_value)
    else:
        loglik = lax.psum_scatter(partial_value, ("row", "col"), scatter_dimension=0, tiled=True)
        posterior = jax.nn.softmax(loglik, axis=1).astype(jnp.bfloat16)
        posterior = lax.all_gather(posterior, ("row", "col"), axis=0, tiled=True)
    expected = jnp.dot(posterior, prob.astype(jnp.bfloat16).T, preferred_element_type=jnp.float32)
    resid = seen * (answered - expected)
    count, total, square = lax.psum(
        (jnp.sum(seen, axis=0), jnp.sum(resid, axis=0), jnp.sum(resid * resid, axis=0)), "lrn"
    )
    count = jnp.maximum(count, 1.0)
    mean = total / count
    var = square / count - mean * mean
    return (seen * (resid - mean) * lax.rsqrt(var + 1e-06) * lax.rsqrt(count)).astype(jnp.bfloat16)


def gram_kernel(planes, z_ref, out_ref, panel, cols, stage, own_sem, out_sem,
                xs, xr, ys, yr, us, ds, zr, ss, sr):
    items = z_ref.shape[0]
    n = items // CHUNK
    r, c, l = lax.axis_index("row"), lax.axis_index("col"), lax.axis_index("lrn")
    plane, core = r // 2, r % 2
    line = c * 2 + l
    source = plane == line
    goes_up = (plane >= line) & (plane < planes - 1)
    goes_down = (plane <= line) & (plane > 0)
    x_to, y_to = (r, c, 1 - l), (r, 1 - c, l)
    up_to, down_to, twin = (r + 2, c, l), (r - 2, c, l), (r + 1 - 2 * core, c, l)

    barrier = pltpu.get_barrier_semaphore()
    for other in (x_to, y_to, twin):
        pl.semaphore_signal(barrier, inc=1, device_id=other, device_id_type=MESH)

    @pl.when(plane < planes - 1)
    def _():
        pl.semaphore_signal(barrier, inc=1, device_id=up_to, device_id_type=MESH)

    @pl.when(plane > 0)
    def _():
        pl.semaphore_signal(barrier, inc=1, device_id=down_to, device_id_type=MESH)

    ends = jnp.where(plane == 0, 1, 0) + jnp.where(plane == planes - 1, 1, 0)
    pl.semaphore_wait(barrier, 5 - ends)

    own = pltpu.make_async_copy(z_ref, panel.at[l, c], own_sem)
    own.start()
    own.wait()

    def rows(i):
        return pl.ds(pl.multiple_of(i * CHUNK, CHUNK), CHUNK)

    def remote(src, dst, send, recv, to):
        return pltpu.make_async_remote_copy(
            src_ref=src, dst_ref=dst, send_sem=send, recv_sem=recv,
            device_id=to, device_id_type=MESH,
        )

    def x_copy(far, i):
        ref = panel.at[l, (1 - c) if far else c, rows(i)]
        at = i + n * far
        return remote(ref, ref, xs.at[at], xr.at[at], x_to)

    def x_wait(far, i):
        ref = panel.at[1 - l, (1 - c) if far else c, rows(i)]
        at = i + n * far
        remote(ref, ref, xs.at[at], xr.at[at], x_to).wait_recv()

    def y_copy(i):
        ref = panel.at[l, c, rows(i)]
        return remote(ref, ref, ys.at[i], yr.at[i], y_to)

    def y_wait(i):
        ref = panel.at[l, 1 - c, rows(i)]
        remote(ref, ref, ys.at[i], yr.at[i], y_to).wait_recv()

    def place(q):
        far, i, cross = q // (2 * n), (q % (2 * n)) // 2, q % 2
        return l + cross - 2 * l * cross, c + far - 2 * c * far, i

    def chunk(which, q):
        px, py, i = place(q)
        return cols.at[which, px, py, rows(i)]

    def up_copy(q):
        return remote(chunk(core, q), chunk(core, q), us.at[q], zr.at[q], up_to)

    def down_copy(q):
        return remote(chunk(core, q), chunk(core, q), ds.at[q], zr.at[q], down_to)

    def twin_copy(q):
        return remote(chunk(core, q), chunk(core, q), ss.at[q], sr.at[q], twin)

    def sent(q):
        @pl.when(goes_up)
        def _():
            up_copy(q).wait_send()

        @pl.when(goes_down)
        def _():
            down_copy(q).wait_send()

        twin_copy(q).wait_send()

    def relay(q):
        @pl.when(source)
        def _():
            px, py, i = place(q)
            move = pltpu.make_async_copy(panel.at[px, py, rows(i)], chunk(core, q), own_sem)
            move.start()
            move.wait()

        @pl.when(jnp.logical_not(source))
        def _():
            up_copy(q).wait_recv()

        @pl.when(q >= AHEAD)
        def _():
            sent(q - AHEAD)

        @pl.when(goes_up)
        def _():
            up_copy(q).start()

        @pl.when(goes_down)
        def _():
            down_copy(q).start()

        twin_copy(q).start()

    def out_copy(slot, start):
        return pltpu.make_async_copy(
            stage.at[slot], out_ref.at[:, pl.ds(pl.multiple_of(start, GROUP), GROUP)],
            out_sem.at[slot],
        )

    def job(p):
        j, part = p // PARTS, p % PARTS
        g, swap, slot = j // 2, j % 2, j % 2
        which = core + swap - 2 * core * swap
        pieces = 2 * GROUP // CHUNK

        @pl.when((swap == 1) & (part == 0))
        def _():
            for s in range(pieces):
                q = pieces * g + s
                remote(chunk(which, q), chunk(which, q), ss.at[q], sr.at[q], twin).wait_recv()

        groups = items // GROUP
        far = g // groups
        py = c + far - 2 * c * far
        base = pl.multiple_of((g % groups) * GROUP, GROUP)

        @pl.when((j >= 2) & (part == 0))
        def _():
            out_copy(slot, 0).wait()

        per = items // TILE

        @pl.loop(0, per)
        def _(m):
            off = pl.multiple_of(m * TILE, TILE)
            acc = None
            for px in range(2):
                term = lax.dot_general(
                    panel[px, part, pl.ds(off, TILE), :],
                    cols[which, px, py, pl.ds(base, GROUP), :],
                    (((1,), (1,)), ((), ())), preferred_element_type=jnp.float32,
                )
                acc = term if acc is None else acc + term
            place_to = pl.ds(pl.multiple_of(part * items + m * TILE, TILE), TILE)
            stage[slot, place_to, :] = acc.astype(stage.dtype)

        @pl.when(part == PARTS - 1)
        def _():
            out_copy(slot, which * 2 * items + py * items + base).start()

    @pl.loop(0, 2 * n)
    def _(q):
        @pl.when(q < n)
        def _():
            x_copy(0, q).start()
            y_copy(q).start()

        @pl.when(q >= n)
        def _():
            y_wait(q - n)
            x_copy(1, q - n).start()

        @pl.when(q % 2 == 1)
        def _():
            x_wait(0, q // 2)

        relay(q)

    @pl.loop(0, n)
    def _(i):
        x_wait(1, i)

    late = 2 * n + 3

    @pl.loop(2 * n, 4 * n)
    def _(q):
        relay(q)

        @pl.when(q >= late)
        def _():
            job(q - late)

    @pl.loop(4 * n - late, PARTS * (4 * items // GROUP))
    def _(p):
        job(p)

    @pl.loop(4 * n - AHEAD, 4 * n)
    def _(q):
        sent(q)

    @pl.loop(0, n)
    def _(i):
        x_copy(0, i).wait_send()
        x_copy(1, i).wait_send()
        y_copy(i).wait_send()

    out_copy(0, 0).wait()
    out_copy(1, 0).wait()


def line_gram(planes, z):
    items, half = z.shape
    n = items // CHUNK
    dma = pltpu.SemaphoreType.DMA
    return pl.pallas_call(
        functools.partial(gram_kernel, planes),
        out_shape=jax.ShapeDtypeStruct((2 * items, 4 * items), jnp.bfloat16),
        in_specs=[pl.BlockSpec(memory_space=pl.ANY)],
        out_specs=pl.BlockSpec(memory_space=pl.ANY),
        scratch_shapes=[
            pltpu.VMEM((2, 2, items, half), jnp.bfloat16),
            pltpu.VMEM((2, 2, 2, items, half), jnp.bfloat16),
            pltpu.VMEM((2, 2 * items, GROUP), jnp.bfloat16),
            dma, dma((2,)),
            dma((2 * n,)), dma((2 * n,)), dma((n,)), dma((n,)),
            dma((4 * n,)), dma((4 * n,)), dma((4 * n,)), dma((4 * n,)), dma((4 * n,)),
        ],
        compiler_params=pltpu.CompilerParams(
            collective_id=0, has_side_effects=True, vmem_limit_bytes=60 * 2**20
        ),
        cost_estimate=pl.CostEstimate(
            flops=2 * 2 * items * 4 * items * 2 * half,
            bytes_accessed=4 * 8 * items * items, transcendentals=0,
        ),
    )(z)


def shards(responses, observed, qmatrix, guess, slip):
    zres = residuals(responses, observed, qmatrix, guess, slip)
    learner_total = zres.shape[0] * lax.axis_size("lrn")
    tiles = lax.axis_size("col") * lax.axis_size("lrn")
    repeats = lax.axis_size("row") // tiles
    if compact():
        zres = with_layout_constraint(zres, Layout(major_to_minor=(0, 1)))
        gram = line_gram(tiles, zres.T)
        return gram.astype(jnp.float32) * jnp.sqrt(jnp.float32(learner_total))
    panel = lax.all_gather(zres, "col", axis=1, tiled=True)
    whole_panel = lax.all_gather(panel, "lrn", axis=0, tiled=True)
    tile_index = lax.axis_index("col") * lax.axis_size("lrn") + lax.axis_index("lrn")
    pieces = [
        spread(whole_panel, "row", tile_index * repeats + offset) for offset in range(repeats)
    ]
    columns = jnp.concatenate(pieces, axis=1)
    gram = learner_product(whole_panel, columns)
    return gram * jnp.sqrt(jnp.float32(learner_total))


def solution(mesh):
    placed = (
        P("lrn", ("row", "col")),
        P("lrn", ("row", "col")),
        P(("row", "col"), None),
        P(("row", "col")),
        P(("row", "col")),
    )
    return jax.shard_map(
        shards, mesh=mesh, in_specs=placed, out_specs=P("row", ("col", "lrn")), check_vma=False
    )
```
